256 devices in a mesh: ctx: 16 (over x_lo, z), head: 16 (over x_hi, y, core).
Axes of the slice: x: 4 (x_hi: 2, x_lo: 2; x = x_hi * 2 + x_lo), y: 4, z: 8, core: 2. Of those that a mesh axis runs over, the one named last changes fastest.
Arguments:
- queries: bfloat16 [4096, 64, 192], P('ctx', 'head'), may hold values from -6 to 6
- latent_cache: bfloat16 [4096, 576], P('ctx'), may hold values from -260 to 260
- key_absorb: bfloat16 [64, 128, 512], P('head'), may hold values from -0.5 to 0.5
- value_absorb: bfloat16 [64, 512, 128], P('head'), may hold values from -0.75 to 0.75
- out_weight: bfloat16 [8192, 7168], P('head'), may hold values from -0.75 to 0.75
- span_order: int32 [32], replicated, may hold values from 0 to 31, as said below
Outputs:
- mixed: bfloat16 [4096, 7168], P('ctx', 'head')
The draws below stay inside these ranges and needn't reach their ends.
Inputs may be any that keep to these rules, and one draw needn't show every extreme that they name: `span_order`: entries 2 d and 2 d + 1 are the spans of device d along ctx; every span number appears once, and the two spans of a device sum to 31.
All inputs are finite; a program needn't handle non-finite values.
Results may differ from the reference program's by a relative error of at most 0.024.
Values may be sent and summed in bfloat16 or wider, within the bound.
No kernel may reach another device: no remote copies, remote signals or barrier semaphores. Data moves between devices by JAX's collectives and lax.ppermute only.
A program may use at most 64 MiB of HBM per device.

```python
import math
import jax
import jax.numpy as jnp
from jax import lax

D = 7168
LATENT = 512
ROPE = 64
NOPE = 128
VHEAD = 128
HEADS = 64
SPAN = 128
SPANS = 32
SEQ = 4096
N_HEAD = 16


def draw_span_order(key, part):
    key = jax.random.fold_in(key, 11)
    pair_key, side_key = jax.random.split(key)
    pair_order = jax.random.permutation(pair_key, SPANS // 2).astype(jnp.int32)
    swapped = jax.random.randint(side_key, (SPANS // 2,), 0, 2)
    lower_ids = pair_order
    upper_ids = SPANS - 1 - pair_order
    leading = jnp.where(swapped == 1, upper_ids, lower_ids)
    trailing = jnp.where(swapped == 1, lower_ids, upper_ids)
    return jnp.stack([leading, trailing], axis=1).reshape(SPANS).astype(jnp.int32)


def draw_latent_cache(key, part):
    key = jax.random.fold_in(key, 5)
    base_key = jax.random.fold_in(key, 0)
    normal_rows = jnp.clip(jax.random.normal(base_key, (SEQ, LATENT + ROPE), jnp.float32), -6.0, 6.0)
    return normal_rows.astype(jnp.bfloat16)


def with_spikes(drawn, stream_key, source, target, shards_of, factor):
    def block_of(axis_at):
        return (jnp.arange(drawn.shape[axis_at]) // (drawn.shape[axis_at] // shards_of)).reshape((-1,) + (1,) * (drawn.ndim - 1 - axis_at))

    near = jax.random.permutation(stream_key, shards_of)[block_of(target)]
    far = (block_of(target) + shards_of // 2) % shards_of
    return jnp.where((block_of(source) == near) | (block_of(source) == far), factor * drawn, drawn)


def level_of(own_key, extent, shards, smallest, largest):
    loudness = 1.0
    for dim, shards_of in shards:
        heights = jax.random.uniform(jax.random.fold_in(jax.random.fold_in(own_key, 6), dim), (shards_of,), jnp.float32, smallest / len(shards), largest / len(shards))
        loudness = loudness * jnp.repeat(jnp.exp(heights), extent[dim] // shards_of).reshape((-1,) + (1,) * (len(extent) - 1 - dim))
    return loudness


def normal_values(own_key, extent, deviation, most, cuts=(), kind=jnp.bfloat16):
    factor_of = level_of(own_key, extent, cuts, -0.22, 0.18) if cuts else 1.0
    entries = jax.random.normal(own_key, extent, jnp.float32) * deviation * factor_of
    return jnp.minimum(jnp.maximum(entries, -most), most).astype(kind)


def noise_with(key, extent, spread, most, cuts, heavy, kind=jnp.bfloat16):
    values = spread * jax.random.normal(key, extent, jnp.float32)
    if cuts:
        values = values * level_of(key, extent, cuts, -0.22, 0.18)
    return jnp.clip(with_spikes(values, jax.random.fold_in(key, 3), *heavy), -most, most).astype(kind)


def setup_inputs(seed: int = 0) -> dict:
    splits = jax.random.split(jax.random.key(seed), 7)
    return {
        "queries": normal_values(splits[0], (SEQ, HEADS, NOPE + ROPE), 1.0, 6.0, ((0, 16), (1, 16))),
        "latent_cache": draw_latent_cache(jax.random.fold_in(splits[6], 71), 0),
        "key_absorb": normal_values(splits[2], (HEADS, NOPE, LATENT), NOPE ** -0.5, 0.5, ((0, 16),)),
        "value_absorb": normal_values(splits[3], (HEADS, LATENT, VHEAD), (LATENT // 8) ** -0.5, 0.75, ((0, 16),)),
        "out_weight": noise_with(splits[4], (HEADS * VHEAD, D), VHEAD ** -0.5, 0.75, ((0, 16),), (0, 1, 16, 2.0)),
        "span_order": draw_span_order(jax.random.fold_in(splits[6], 71), 0),
    }


def rotate(values, angle_pos):
    half_width = values.shape[-1] // 2
    inverse = 10000.0 ** (-jnp.arange(half_width, dtype=jnp.float32) * 2.0 / values.shape[-1])
    angles = angle_pos.astype(jnp.float32)[..., None] * inverse
    front_half = values[..., :half_width]
    back_half = values[..., half_width:]
    cosine = jnp.cos(angles)
    sine_part = jnp.sin(angles)
    return jnp.concatenate([front_half * cosine - back_half * sine_part, front_half * sine_part + back_half * cosine], axis=-1)

def reference(queries, latent_cache, key_absorb, value_absorb, out_weight, span_order):
    row_index = jnp.arange(SEQ, dtype=jnp.int32)
    token_pos = (span_order[row_index // SPAN] * SPAN + row_index % SPAN).astype(jnp.int32)
    rotated = rotate(latent_cache[:, LATENT:].astype(jnp.float32), token_pos).astype(jnp.bfloat16)
    keys = jnp.concatenate([latent_cache[:, :LATENT], rotated], axis=1)
    query_latent = jnp.einsum('thn,hnl->thl', queries[:, :, :NOPE].astype(jnp.float32), key_absorb.astype(jnp.float32)).astype(jnp.bfloat16)
    query_rope = rotate(queries[:, :, NOPE:].astype(jnp.float32), token_pos[:, None]).astype(jnp.bfloat16)
    absorbed = jnp.concatenate([query_latent, query_rope], axis=2)
    score_scale = 1.0 / math.sqrt(NOPE + ROPE)
    keys_wide = keys.astype(jnp.float32)
    visible = token_pos[None, :] <= token_pos[:, None]

    def one_head(query_rows):
        scores = jnp.dot(query_rows.astype(jnp.float32), keys_wide.T, preferred_element_type=jnp.float32) * score_scale
        scores = jnp.where(visible, scores, -jnp.inf)
        weights = lax.optimization_barrier(jax.nn.softmax(scores, axis=1).astype(jnp.bfloat16))
        summed = jnp.dot(weights.astype(jnp.float32), keys_wide[:, :LATENT], preferred_element_type=jnp.float32)
        return summed.astype(jnp.bfloat16)
    context = lax.map(one_head, jnp.transpose(absorbed, (1, 0, 2)))
    head_values = jnp.einsum('hsl,hlv->shv', context.astype(jnp.float32), value_absorb.astype(jnp.float32)).astype(jnp.bfloat16)
    group_heads = HEADS // N_HEAD
    flat_values = jnp.transpose(head_values.reshape(SEQ, N_HEAD, group_heads * VHEAD), (1, 0, 2))
    grouped_weight = out_weight.reshape(N_HEAD, group_heads * VHEAD, D)

    def add_group(running, members):
        group_values, group_weight = members
        term = jnp.dot(group_values.astype(jnp.float32), group_weight.astype(jnp.float32), preferred_element_type=jnp.float32)
        term = lax.optimization_barrier(term.astype(jnp.bfloat16))
        return (running + term.astype(jnp.float32), None)
    summed = lax.scan(add_group, jnp.zeros((SEQ, D), jnp.float32), (flat_values, grouped_weight))[0]
    return summed.astype(jnp.bfloat16)
```

```python
import functools
import math

import jax
import jax.numpy as jnp
import numpy as np
from jax import lax
from jax.experimental import pallas as pl
from jax.experimental.pallas import tpu as pltpu
from jax.sharding import PartitionSpec as P

BF16 = jnp.bfloat16
F32 = jnp.float32
AXES = ("ctx", "head")
NXL, NZ, NXH, NY, NC = 2, 8, 2, 4, 2
SPAN = 128
LAT = 512
ROPE = 64
PIECE = 144
HEADS = 4
NEG = -1e30
VMEM = pltpu.CompilerParams(vmem_limit_bytes=56 * 1024 * 1024)


def device(x, y, z, c):
    x, y, z = x % 4, y % NY, z % NZ
    return ((((x % 2) * NZ + z) * NXH + x // 2) * NY + y) * NC + c


def routes(step):
    pairs = []
    for x in range(4):
        for y in range(NY):
            for z in range(NZ):
                for c in range(NC):
                    pairs.append((device(x, y, z, c), device(*step(x, y, z, c))))
    return pairs


def way(c):
    return 1 - 2 * c


def send(value, step):
    return lax.ppermute(value, AXES, routes(step))


def along(dx=0, dy=0, dz=0):
    return lambda x, y, z, c: (x + dx * way(c), y + dy * way(c), z + dz * way(c), c)


def swap(x, y, z, c):
    return x, y, z, 1 - c


def tables():
    inverse = 10000.0 ** (-np.arange(ROPE // 2, dtype=np.float64) * 2.0 / ROPE)
    inverse = np.concatenate([inverse, inverse])[None, :]
    sign = np.concatenate([-np.ones(ROPE // 2), np.ones(ROPE // 2)])[None, :]
    rows = np.arange(SPAN, dtype=np.float64)[:, None] * inverse
    spans = np.arange(32, dtype=np.float64)[:, None] * SPAN * inverse
    table = np.concatenate(
        [
            np.concatenate([np.cos(rows), sign * np.sin(rows)], axis=1),
            np.concatenate([np.cos(spans), sign * np.sin(spans)], axis=1),
        ],
        axis=0,
    ).astype(np.float32)
    swapper = np.roll(np.eye(ROPE, dtype=np.float32), ROPE // 2, axis=1)
    return jnp.asarray(table), jnp.asarray(swapper, dtype=BF16)


def cos_sin(table_ref, span):
    cr, sr = table_ref[0:SPAN, 0:ROPE], table_ref[0:SPAN, ROPE : 2 * ROPE]
    row = table_ref[pl.ds(SPAN + span, 1), :]
    cs, ss = row[:, 0:ROPE], row[:, ROPE : 2 * ROPE]
    return cr * cs - sr * ss, cr * ss + sr * cs


def rotated(values, cos, sin, swapper):
    other = jnp.dot(values, swapper, preferred_element_type=F32)
    return values.astype(F32) * cos + other * sin


def me():
    ctx, head = lax.axis_index("ctx"), lax.axis_index("head")
    return ctx // NZ, ctx % NZ, head // (NY * NC), (head // NC) % NY, head % NC


def span_of(order_ref, xl, z, half):
    ctx = xl * NZ + lax.rem(z + 2 * NZ, NZ)
    a, b = order_ref[2 * ctx], order_ref[2 * ctx + 1]
    return jnp.where(half == 0, jnp.minimum(a, b), jnp.maximum(a, b))


def own_rows(order_ref, half):
    ctx = lax.axis_index("ctx")
    swapped = (order_ref[2 * ctx] > order_ref[2 * ctx + 1]).astype(jnp.int32)
    return pl.multiple_of(SPAN * (swapped ^ half), SPAN)


SMEM_SPEC = pl.BlockSpec(memory_space=pltpu.SMEM)
VMEM_SPEC = pl.BlockSpec(memory_space=pltpu.VMEM)
ANY_SPEC = pl.BlockSpec(memory_space=pl.ANY)


def pack_kernel(order_ref, cache_ref, table_ref, swapper_ref, own_ref, slice_ref, first_ref):
    xl, z, xh, y, c = me()
    for half in range(2):
        rows = own_rows(order_ref, half)
        span = span_of(order_ref, xl, z, half)
        latent = cache_ref[pl.ds(rows, SPAN), 0:LAT]
        raw = cache_ref[pl.ds(rows, SPAN), LAT : LAT + ROPE]
        cos, sin = cos_sin(table_ref, span)
        turned = rotated(raw, cos, sin, swapper_ref[...])
        tiles = [
            jnp.concatenate(
                [turned[32 * j : 32 * j + 16], turned[32 * j + 16 : 32 * j + 32]], axis=1
            )
            for j in range(4)
        ]
        packed = jnp.concatenate(tiles, axis=1).astype(BF16)
        own_ref[half, 0:SPAN, :] = latent
        own_ref[half, SPAN:PIECE, :] = packed

        @pl.when(y % 2 == half)
        def _():
            slice_ref[0:SPAN, :] = latent
            slice_ref[SPAN:PIECE, :] = packed

        @pl.when(c == half)
        def _():
            first_ref[0:SPAN, :] = latent
            first_ref[SPAN:PIECE, :] = packed


def pack(order, cache, table, swapper):
    return pl.pallas_call(
        pack_kernel,
        out_shape=(
            jax.ShapeDtypeStruct((2, PIECE, LAT), BF16),
            jax.ShapeDtypeStruct((PIECE, LAT), BF16),
            jax.ShapeDtypeStruct((PIECE, LAT), BF16),
        ),
        in_specs=[SMEM_SPEC, VMEM_SPEC, VMEM_SPEC, VMEM_SPEC],
        out_specs=(VMEM_SPEC,) * 3,
        compiler_params=VMEM,
        name="pack_keys",
    )(order, cache, table, swapper)


def absorb_kernel(order_ref, query_ref, absorb_ref, table_ref, swapper_ref, out_ref):
    xl, z, xh, y, c = me()
    for half in range(2):
        rows = own_rows(order_ref, half)
        cos, sin = cos_sin(table_ref, span_of(order_ref, xl, z, half))
        for h in range(HEADS):
            q = query_ref[h, pl.ds(rows, SPAN), :]
            nope, raw = q[:, 0:128], q[:, 128:192]
            part = jnp.dot(nope, absorb_ref[h], preferred_element_type=F32).astype(BF16)
            turned = rotated(raw, cos, sin, swapper_ref[...])
            tail = jnp.concatenate([turned, jnp.zeros_like(turned)], axis=1).astype(BF16)
            out_ref[half, h * SPAN : (h + 1) * SPAN, 0:LAT] = part
            out_ref[half, h * SPAN : (h + 1) * SPAN, LAT : LAT + 128] = tail


def absorb(order, queries, key_absorb, table, swapper):
    return pl.pallas_call(
        absorb_kernel,
        out_shape=jax.ShapeDtypeStruct((2, HEADS * SPAN, LAT + 128), BF16),
        in_specs=[SMEM_SPEC] + [VMEM_SPEC] * 4,
        out_specs=VMEM_SPEC,
        compiler_params=VMEM,
        name="absorb_queries",
    )(order, queries, key_absorb, table, swapper)


def attend_kernel(
    order_ref, q_ref, va_ref, own, first, b12, y12, x12, d12, b3, y3, x3, d3, b4, y4, x4, d4, g1, g2,
    out_ref, keys, krope, scores, peak, total, acc, sems,
):
    xl, z, xh, y, c = me()
    s = y % 2
    w = 1 - 2 * c
    copies = []

    def fetch(src, dst):
        copy = pltpu.make_async_copy(src, dst, sems.at[len(copies)])
        copy.start()
        copies.append(copy)

    for half in range(2):
        fetch(own.at[half], keys.at[span_of(order_ref, xl, z, half)])
    fetch(first, keys.at[span_of(order_ref, 1 - xl, z, c)])
    fetch(g1.at[pl.ds(0, PIECE)], keys.at[span_of(order_ref, 1 - xl, z, 1 - c)])
    kinds = ((xl, s), (xl, 1 - s), (1 - xl, s), (1 - xl, 1 - s))
    for k, (bundle, third, fourth) in enumerate(((b12, b3, b4), (y12, y3, y4), (x12, x3, x4), (d12, d3, d4))):
        px, ph = kinds[k]
        for t in (1, 2):
            here = span_of(order_ref, px, z - w * t, ph)
            there = span_of(order_ref, px, z + w * t, ph)
            fetch(bundle.at[pl.ds((t - 1) * PIECE, PIECE)], keys.at[here])
            fetch(g1.at[pl.ds((1 + 2 * k + t - 1) * PIECE, PIECE)], keys.at[there])
        fetch(third, keys.at[span_of(order_ref, px, z - 3 * w, ph)])
        fetch(g2.at[pl.ds(k * PIECE, PIECE)], keys.at[span_of(order_ref, px, z + 3 * w, ph)])
        far = span_of(order_ref, px, z + 4, ph)
        mine = pl.multiple_of(256 * c, 256)
        other = pl.multiple_of(256 * (1 - c), 256)
        fetch(fourth, keys.at[far, :, pl.ds(mine, 256)])
        fetch(
            g2.at[pl.ds((4 + k // 2) * PIECE, PIECE), pl.ds(256 * (k % 2), 256)],
            keys.at[far, :, pl.ds(other, 256)],
        )
    for copy in copies:
        copy.wait()

    def unpack(i, _):
        packed = keys[i, SPAN:PIECE, :].astype(F32)
        zero = jnp.zeros((16, ROPE), F32)
        for j in range(8):
            part = jnp.concatenate([packed[:, ROPE * j : ROPE * (j + 1)], zero], axis=1)
            krope[pl.ds(pl.multiple_of(i * SPAN + 16 * j, 16), 16), :] = part.astype(BF16)
        return 0

    lax.fori_loop(0, 32, unpack, 0, unroll=4)

    lower = span_of(order_ref, xl, z, 0)
    upper = 31 - lower
    count = lower // 2
    scale = math.log2(math.e) / math.sqrt(192.0)
    wide = (((1,), (1,)), ((), ()))

    def score(half, block):
        latent = keys[pl.ds(2 * block, 2), 0:SPAN, :].reshape(2 * SPAN, LAT)
        turned = krope[pl.ds(pl.multiple_of(block * 2 * SPAN, 2 * SPAN), 2 * SPAN), :]
        q = q_ref[half]
        return lax.dot_general(q[:, 0:LAT], latent, wide, preferred_element_type=F32) + lax.dot_general(
            q[:, LAT:], turned, wide, preferred_element_type=F32
        )

    for half, span in ((0, lower), (1, upper)):
        block = span // 2
        value = score(half, block)
        row = lax.rem(lax.broadcasted_iota(jnp.int32, value.shape, 0), SPAN) + (span % 2) * SPAN
        column = lax.broadcasted_iota(jnp.int32, value.shape, 1)
        value = jnp.where(column <= row, value, NEG)
        scores[15 + half] = value
        peak[half] = jnp.maximum(value[:, 0:128], value[:, 128:256])

    def place(i):
        half = (i >= count).astype(jnp.int32)
        return half, i - half * count

    def first_pass(i, _):
        half, block = place(i)
        value = score(half, block)
        scores[i] = value
        peak[half] = jnp.maximum(peak[half], jnp.maximum(value[:, 0:128], value[:, 128:256]))
        return 0

    lax.fori_loop(0, 15, first_pass, 0)
    for half in range(2):
        top = jnp.max(peak[half], axis=1, keepdims=True) * scale
        peak[half] = jnp.broadcast_to(top, (HEADS * SPAN, 128))

    def weigh(i, half, block):
        top = peak[half]
        value = scores[i]
        left = jnp.exp2(value[:, 0:128] * scale - top)
        right = jnp.exp2(value[:, 128:256] * scale - top)
        weights = jnp.concatenate([left.astype(BF16), right.astype(BF16)], axis=1)
        latent = keys[pl.ds(2 * block, 2), 0:SPAN, :].reshape(2 * SPAN, LAT)
        return left + right, jnp.dot(weights, latent, preferred_element_type=F32)

    for half, span in ((0, lower), (1, upper)):
        some, product = weigh(15 + half, half, span // 2)
        total[half] = some
        acc[half] = product

    def second_pass(i, _):
        half, block = place(i)
        some, product = weigh(i, half, block)
        total[half] += some
        acc[half] += product
        return 0

    lax.fori_loop(0, 15, second_pass, 0)

    for half in range(2):
        rows = own_rows(order_ref, half)
        for h in range(HEADS):
            part = slice(h * SPAN, (h + 1) * SPAN)
            bottom = jnp.sum(total[half, part, :], axis=1, keepdims=True)
            context = (acc[half, part, :] / bottom).astype(BF16)
            value = jnp.dot(context, va_ref[h], preferred_element_type=F32)
            out_ref[pl.ds(rows, SPAN), h * 128 : (h + 1) * 128] = value.astype(BF16)


def attend(order, q, value_absorb, pieces):
    return pl.pallas_call(
        attend_kernel,
        out_shape=jax.ShapeDtypeStruct((2 * SPAN, HEADS * 128), BF16),
        in_specs=[SMEM_SPEC, VMEM_SPEC, VMEM_SPEC] + [ANY_SPEC] * len(pieces),
        out_specs=VMEM_SPEC,
        scratch_shapes=[
            pltpu.VMEM((32, PIECE, LAT), BF16),
            pltpu.VMEM((32 * SPAN, 128), BF16),
            pltpu.VMEM((17, HEADS * SPAN, 2 * SPAN), F32),
            pltpu.VMEM((2, HEADS * SPAN, 128), F32),
            pltpu.VMEM((2, HEADS * SPAN, 128), F32),
            pltpu.VMEM((2, HEADS * SPAN, LAT), F32),
            pltpu.SemaphoreType.DMA((48,)),
        ],
        compiler_params=VMEM,
        cost_estimate=pl.CostEstimate(flops=6_000_000_000, bytes_accessed=8_000_000, transcendentals=2_200_000),
        name="attend",
    )(order, q, value_absorb, *pieces)


def columns_kernel(weight_ref, keep_ref, give_ref):
    c = lax.axis_index("head") % NC
    left = weight_ref[:, 0:448]
    right = weight_ref[:, 448:896]

    @pl.when(c == 0)
    def _():
        keep_ref[0] = left
        give_ref[0] = right

    @pl.when(c == 1)
    def _():
        keep_ref[0] = right
        give_ref[0] = left


def split_columns(weight):
    rows = weight.shape[0]
    return pl.pallas_call(
        columns_kernel,
        grid=(8,),
        out_shape=(jax.ShapeDtypeStruct((8, rows, 448), BF16),) * 2,
        in_specs=[pl.BlockSpec((rows, 896), lambda k: (0, k))],
        out_specs=(pl.BlockSpec((1, rows, 448), lambda k: (k, 0, 0)),) * 2,
        compiler_params=VMEM,
        cost_estimate=pl.CostEstimate(flops=0, bytes_accessed=15_000_000, transcendentals=0),
        name="split_columns",
    )(weight)


OFFSETS = [(1, 2), (1, 1), (1, 3), (0, 2), (1, 0), (0, 1), (0, 3), (0, 0)]


def project_kernel(own_ref, other_ref, keep_ref, got_ref, *rest):
    outs, (keep, got, sems) = rest[:8], rest[8:]
    xl, z, xh, y, c = me()
    copies = []
    for r, (dx, dy) in enumerate(OFFSETS):
        k = lax.rem(xh + dx, NXH) * NY + lax.rem(y + dy, NY)
        pair = (
            pltpu.make_async_copy(keep_ref.at[k], keep.at[r], sems.at[0, r]),
            pltpu.make_async_copy(got_ref.at[k], got.at[r], sems.at[1, r]),
        )
        for copy in pair:
            copy.start()
        copies.append(pair)
    for r in range(8):
        for copy in copies[r]:
            copy.wait()
        outs[r][...] = (
            jnp.dot(own_ref[...], keep[r], preferred_element_type=F32)
            + jnp.dot(other_ref[...], got[r], preferred_element_type=F32)
        ).astype(BF16)


def project(own, other, keep, got):
    rows = own.shape[0]
    return pl.pallas_call(
        project_kernel,
        out_shape=(jax.ShapeDtypeStruct((rows, 448), BF16),) * 8,
        in_specs=[VMEM_SPEC, VMEM_SPEC, ANY_SPEC, ANY_SPEC],
        out_specs=(VMEM_SPEC,) * 8,
        scratch_shapes=[
            pltpu.VMEM((8, 512, 448), BF16),
            pltpu.VMEM((8, 512, 448), BF16),
            pltpu.SemaphoreType.DMA((2, 8)),
        ],
        compiler_params=VMEM,
        cost_estimate=pl.CostEstimate(flops=1_900_000_000, bytes_accessed=8_000_000, transcendentals=0),
        name="project",
    )(own, other, keep, got)


def body(queries, latent_cache, key_absorb, value_absorb, out_weight, span_order):
    table, swapper = tables()
    own, piece, first_half = pack(span_order, latent_cache, table, swapper)

    first = send(first_half, along(dx=1))
    c = lax.axis_index("head") % NC
    columns = jnp.where(c == 0, piece[:, 0:256], piece[:, 256:512])
    b1 = send(piece, along(dz=1))
    b2 = send(piece, along(dz=2))
    b3 = send(piece, along(dz=3))
    b4 = send(columns, along(dz=4))
    b12 = jnp.concatenate([b1, b2], axis=0)
    ways = (along(dy=1), along(dx=1), along(dx=1, dy=1))
    y12, x12, d12 = (send(b12, step) for step in ways)
    y3, x3, d3 = (send(b3, step) for step in ways)
    y4, x4, d4 = (send(b4, step) for step in ways)
    g1 = send(jnp.concatenate([first, b12, y12, x12, d12], axis=0), swap)
    g2 = send(
        jnp.concatenate(
            [b3, y3, x3, d3, jnp.concatenate([b4, y4], axis=1), jnp.concatenate([x4, d4], axis=1)], axis=0
        ),
        swap,
    )

    q = absorb(span_order, queries.transpose(1, 0, 2), key_absorb, table, swapper)
    keep, give = split_columns(out_weight)
    got = send(give, swap)
    pieces = (own, first, b12, y12, x12, d12, b3, y3, x3, d3, b4, y4, x4, d4, g1, g2)
    values = attend(span_order, q, value_absorb, pieces)
    other = send(values, swap)
    terms = project(values, other, keep, got)
    landed = [
        term if (dx, dy) == (0, 0) else send(term, lambda x, y, z, c, dx=dx, dy=dy: (x + 2 * dx, y + dy, z, c))
        for term, (dx, dy) in zip(terms, OFFSETS)
    ]
    return functools.reduce(jnp.add, [term.astype(F32) for term in landed]).astype(BF16)


def solution(mesh):
    return jax.shard_map(
        body,
        mesh=mesh,
        in_specs=(
            P("ctx", "head", None),
            P("ctx", None),
            P("head", None, None),
            P("head", None, None),
            P("head", None),
            P(),
        ),
        out_specs=P("ctx", "head"),
        check_vma=False,
    )
```

```python
import functools
import math

import jax
import jax.numpy as jnp
import numpy as np
from jax import lax
from jax.experimental import pallas as pl
from jax.experimental.pallas import tpu as pltpu
from jax.sharding import PartitionSpec as P

BF16 = jnp.bfloat16
F32 = jnp.float32
AXES = ("ctx", "head")
NXL, NZ, NXH, NY, NC = 2, 8, 2, 4, 2
SPAN = 128
LAT = 512
ROPE = 64
KEY = LAT + ROPE
HEADS = 4
NEG = -1e30
MIB = 1024 * 1024


def vmem(mib):
    return pltpu.CompilerParams(vmem_limit_bytes=mib * MIB)


def device(x, y, z, c):
    x, y, z = x % 4, y % NY, z % NZ
    return ((((x % 2) * NZ + z) * NXH + x // 2) * NY + y) * NC + c


def routes(step):
    pairs = []
    for x in range(4):
        for y in range(NY):
            for z in range(NZ):
                for c in range(NC):
                    pairs.append((device(x, y, z, c), device(*step(x, y, z, c))))
    return pairs


def way(c):
    return 1 - 2 * c


def send(value, step):
    return lax.ppermute(value, AXES, routes(step))


def along(dx=0, dy=0, dz=0):
    return lambda x, y, z, c: (x + dx * way(c), y + dy * way(c), z + dz * way(c), c)


def swap(x, y, z, c):
    return x, y, z, 1 - c


def tables():
    inverse = 10000.0 ** (-np.arange(ROPE // 2, dtype=np.float64) * 2.0 / ROPE)[:, None]
    rows = inverse * np.arange(SPAN, dtype=np.float64)[None, :]
    spans = inverse * SPAN * np.arange(SPAN, dtype=np.float64)[None, :]
    return jnp.asarray(np.stack([np.cos(rows), np.sin(rows), np.cos(spans), np.sin(spans)]).astype(np.float32))


def cos_sin(table_ref, span):
    here = lax.broadcasted_iota(jnp.int32, (ROPE // 2, SPAN), 1) == span
    cs = jnp.sum(jnp.where(here, table_ref[2], 0.0), axis=1, keepdims=True)
    ss = jnp.sum(jnp.where(here, table_ref[3], 0.0), axis=1, keepdims=True)
    cr, sr = table_ref[0], table_ref[1]
    return cr * cs - sr * ss, cr * ss + sr * cs


def rotated(values, cos, sin):
    front, back = values[0:32].astype(F32), values[32:64].astype(F32)
    return jnp.concatenate([front * cos - back * sin, front * sin + back * cos], axis=0)


def me():
    ctx, head = lax.axis_index("ctx"), lax.axis_index("head")
    return ctx // NZ, ctx % NZ, head // (NY * NC), (head // NC) % NY, head % NC


def span_of(order_ref, xl, z, half):
    ctx = xl * NZ + lax.rem(z + 2 * NZ, NZ)
    a, b = order_ref[2 * ctx], order_ref[2 * ctx + 1]
    return jnp.where(half == 0, jnp.minimum(a, b), jnp.maximum(a, b))


def own_rows(order_ref, half):
    ctx = lax.axis_index("ctx")
    swapped = (order_ref[2 * ctx] > order_ref[2 * ctx + 1]).astype(jnp.int32)
    return pl.multiple_of(SPAN * (swapped ^ half), SPAN)


SMEM_SPEC = pl.BlockSpec(memory_space=pltpu.SMEM)
VMEM_SPEC = pl.BlockSpec(memory_space=pltpu.VMEM)
ANY_SPEC = pl.BlockSpec(memory_space=pl.ANY)


def pack_kernel(order_ref, cache_ref, table_ref, own_ref, slice_ref, part_ref, first_ref):
    xl, z, xh, y, c = me()
    for half in range(2):
        tokens = pl.ds(own_rows(order_ref, half), SPAN)
        cos, sin = cos_sin(table_ref, span_of(order_ref, xl, z, half))
        own_ref[half, 0:LAT, :] = cache_ref[0:LAT, tokens]
        own_ref[half, LAT:KEY, :] = rotated(cache_ref[LAT:KEY, tokens], cos, sin).astype(BF16)
    slice_ref[...] = own_ref[y % 2]
    part_ref[...] = own_ref[y % 2, pl.ds(pl.multiple_of(c * (KEY // 2), 32), KEY // 2), :]
    first_ref[...] = own_ref[c]


def pack(order, cache, table):
    return pl.pallas_call(
        pack_kernel,
        out_shape=(
            jax.ShapeDtypeStruct((2, KEY, SPAN), BF16),
            jax.ShapeDtypeStruct((KEY, SPAN), BF16),
            jax.ShapeDtypeStruct((KEY // 2, SPAN), BF16),
            jax.ShapeDtypeStruct((KEY, SPAN), BF16),
        ),
        in_specs=[SMEM_SPEC, VMEM_SPEC, VMEM_SPEC],
        out_specs=(VMEM_SPEC,) * 4,
        compiler_params=vmem(16),
        name="pack_keys",
    )(order, cache, table)


def absorb_kernel(order_ref, query_ref, absorb_ref, table_ref, out_ref):
    xl, z, xh, y, c = me()
    for half in range(2):
        tokens = pl.ds(own_rows(order_ref, half), SPAN)
        cos, sin = cos_sin(table_ref, span_of(order_ref, xl, z, half))
        for h in range(HEADS):
            rows = slice(h * SPAN, (h + 1) * SPAN)
            nope = query_ref[h, 0:128, tokens].T
            part = jnp.dot(nope, absorb_ref[h], preferred_element_type=F32)
            out_ref[half, rows, 0:LAT] = part.astype(BF16)
            turned = rotated(query_ref[h, 128:192, tokens], cos, sin)
            out_ref[half, rows, LAT:KEY] = turned.T.astype(BF16)


def absorb(order, queries, key_absorb, table):
    return pl.pallas_call(
        absorb_kernel,
        out_shape=jax.ShapeDtypeStruct((2, HEADS * SPAN, KEY), BF16),
        in_specs=[SMEM_SPEC] + [VMEM_SPEC] * 3,
        out_specs=VMEM_SPEC,
        compiler_params=vmem(16),
        name="absorb_queries",
    )(order, queries, key_absorb, table)


BLOCK = 4
STEPS = 7


def attend_kernel(
    order_ref, q_ref, va_ref, own, first, first2, bb, yy, xx, dd, bb2, yy2, xx2, dd2,
    out_ref, keys, scores, peaks, total, acc, sems,
):
    xl, z, xh, y, c = me()
    s = y % 2
    w = 1 - 2 * c
    copies = []

    def fetch(src, dst):
        copy = pltpu.make_async_copy(src, dst, sems.at[len(copies)])
        copy.start()
        copies.append(copy)

    for half in range(2):
        fetch(own.at[half], keys.at[span_of(order_ref, xl, z, half)])
    fetch(first, keys.at[span_of(order_ref, 1 - xl, z, c)])
    fetch(first2, keys.at[span_of(order_ref, 1 - xl, z, 1 - c)])
    kinds = ((xl, s), (xl, 1 - s), (1 - xl, s), (1 - xl, 1 - s))
    for (px, ph), mine, other in zip(kinds, (bb, yy, xx, dd), (bb2, yy2, xx2, dd2)):
        for t in (1, 2, 3):
            rows = pl.ds((t - 1) * KEY, KEY)
            fetch(mine.at[rows], keys.at[span_of(order_ref, px, z - w * t, ph)])
            fetch(other.at[rows], keys.at[span_of(order_ref, px, z + w * t, ph)])
        far = span_of(order_ref, px, z + 4, ph)
        rows = pl.ds(3 * KEY, KEY // 2)
        fetch(mine.at[rows], keys.at[far, pl.ds(pl.multiple_of(KEY // 2 * c, 32), KEY // 2)])
        fetch(other.at[rows], keys.at[far, pl.ds(pl.multiple_of(KEY // 2 * (1 - c), 32), KEY // 2)])
    for copy in copies:
        copy.wait()

    lower = span_of(order_ref, xl, z, 0)
    upper = 31 - lower
    count = lower // BLOCK
    scale = math.log2(math.e) / math.sqrt(192.0)
    wide = BLOCK * SPAN

    def tokens(block, rows):
        return jnp.concatenate([keys[BLOCK * block + i, rows, :] for i in range(BLOCK)], axis=1)

    def score(half, block):
        latent = jnp.dot(q_ref[half, :, 0:LAT], tokens(block, slice(0, LAT)), preferred_element_type=F32)
        turned = jnp.dot(q_ref[half, :, LAT:KEY], tokens(block, slice(LAT, KEY)), preferred_element_type=F32)
        return latent + turned

    def widest(value):
        parts = [value[:, 128 * i : 128 * (i + 1)] for i in range(BLOCK)]
        return jnp.maximum(jnp.maximum(parts[0], parts[1]), jnp.maximum(parts[2], parts[3]))

    def place(i):
        half = (i >= count).astype(jnp.int32)
        return half, i - half * count

    for half, span in ((0, lower), (1, upper)):
        value = score(half, span // BLOCK)
        row = lax.broadcasted_iota(jnp.int32, value.shape, 0) % SPAN + (span % BLOCK) * SPAN
        column = lax.broadcasted_iota(jnp.int32, value.shape, 1)
        value = jnp.where(column <= row, value, NEG)
        scores[STEPS + half] = value
        peaks[STEPS + half] = widest(value)
    for i in range(STEPS):
        value = score(*place(i))
        scores[i] = value
        peaks[i] = widest(value)

    for half in range(2):
        top = peaks[STEPS + half]
        for i in range(STEPS):
            top = jnp.where(place(i)[0] == half, jnp.maximum(top, peaks[i]), top)
        top = jnp.max(top, axis=1, keepdims=True) * scale
        peaks[STEPS + half] = jnp.broadcast_to(top, top.shape[:1] + (128,))

    def weigh(i, half, block):
        top = peaks[STEPS + half]
        parts = [jnp.exp2(scores[i, :, 128 * j : 128 * (j + 1)] * scale - top) for j in range(BLOCK)]
        weights = jnp.concatenate([part.astype(BF16) for part in parts], axis=1)
        product = lax.dot_general(
            weights, tokens(block, slice(0, LAT)), (((1,), (1,)), ((), ())), preferred_element_type=F32
        )
        return (parts[0] + parts[1]) + (parts[2] + parts[3]), product

    for half, span in ((0, lower), (1, upper)):
        total[half], acc[half] = weigh(STEPS + half, half, span // BLOCK)
    for i in range(STEPS):
        half, block = place(i)
        some, product = weigh(i, half, block)
        total[half] += some
        acc[half] += product

    for half in range(2):
        rows = own_rows(order_ref, half)
        for h in range(HEADS):
            part = slice(h * SPAN, (h + 1) * SPAN)
            bottom = jnp.sum(total[half, part, :], axis=1, keepdims=True)
            context = (acc[half, part, :] / bottom).astype(BF16)
            value = jnp.dot(context, va_ref[h], preferred_element_type=F32)
            out_ref[pl.ds(rows, SPAN), h * 128 : (h + 1) * 128] = value.astype(BF16)


def attend(order, q, value_absorb, pieces):
    rows = HEADS * SPAN
    return pl.pallas_call(
        attend_kernel,
        out_shape=jax.ShapeDtypeStruct((2 * SPAN, HEADS * 128), BF16),
        in_specs=[SMEM_SPEC, VMEM_SPEC, VMEM_SPEC] + [ANY_SPEC] * len(pieces),
        out_specs=VMEM_SPEC,
        scratch_shapes=[
            pltpu.VMEM((32, KEY, SPAN), BF16),
            pltpu.VMEM((STEPS + 2, rows, BLOCK * SPAN), F32),
            pltpu.VMEM((STEPS + 2, rows, 128), F32),
            pltpu.VMEM((2, rows, 128), F32),
            pltpu.VMEM((2, rows, LAT), F32),
            pltpu.SemaphoreType.DMA((40,)),
        ],
        compiler_params=vmem(40),
        cost_estimate=pl.CostEstimate(flops=6_000_000_000, bytes_accessed=8_000_000, transcendentals=2_200_000),
        name="attend",
    )(order, q, value_absorb, *pieces)


def columns_kernel(weight_ref, wait_ref, keep_ref, give_ref):
    c = lax.axis_index("head") % NC
    turned = weight_ref[...].T

    @pl.when(c == 0)
    def _():
        keep_ref[...] = turned[0:448]
        give_ref[...] = turned[448:896]

    @pl.when(c == 1)
    def _():
        keep_ref[...] = turned[448:896]
        give_ref[...] = turned[0:448]


def split_columns(weight, wait):
    rows = weight.shape[0]
    return pl.pallas_call(
        columns_kernel,
        grid=(8,),
        out_shape=(jax.ShapeDtypeStruct((8 * 448, rows), BF16),) * 2,
        in_specs=[pl.BlockSpec((rows, 896), lambda k: (0, k)), ANY_SPEC],
        out_specs=(pl.BlockSpec((448, rows), lambda k: (k, 0)),) * 2,
        compiler_params=vmem(24),
        cost_estimate=pl.CostEstimate(flops=0, bytes_accessed=15_000_000, transcendentals=0),
        name="split_columns",
    )(weight, wait)


OFFSETS = [(1, 2), (1, 1), (1, 3), (0, 2), (1, 0), (0, 1), (0, 3), (0, 0)]


def project_kernel(own_ref, other_ref, keep_ref, got_ref, *outs):
    xl, z, xh, y, c = me()
    contract = (((1,), (1,)), ((), ()))
    for out_ref, (dx, dy) in zip(outs, OFFSETS):
        k = lax.rem(xh + dx, NXH) * NY + lax.rem(y + dy, NY)
        rows = pl.ds(pl.multiple_of(k * 448, 64), 448)
        term = lax.dot_general(keep_ref[rows, :], own_ref[...], contract, preferred_element_type=F32)
        term += lax.dot_general(got_ref[rows, :], other_ref[...], contract, preferred_element_type=F32)
        out_ref[...] = term.astype(BF16)


def project(own, other, keep, got):
    return pl.pallas_call(
        project_kernel,
        out_shape=(jax.ShapeDtypeStruct((448, 256), BF16),) * 8,
        in_specs=[VMEM_SPEC] * 4,
        out_specs=(VMEM_SPEC,) * 8,
        compiler_params=vmem(24),
        cost_estimate=pl.CostEstimate(flops=1_900_000_000, bytes_accessed=8_000_000, transcendentals=0),
        name="project",
    )(own, other, keep, got)


def body(queries, latent_cache, key_absorb, value_absorb, out_weight, span_order):
    table = tables()
    own, piece, part, first_half = pack(span_order, latent_cache.T, table)

    b1 = send(piece, along(dz=1))
    b2 = send(piece, along(dz=2))
    b3 = send(piece, along(dz=3))
    b4 = send(part, along(dz=4))
    first = send(first_half, along(dx=1))
    keep, give = split_columns(out_weight, piece)
    bb, give, first = lax.optimization_barrier((jnp.concatenate([b1, b2, b3, b4], axis=0), give, first))
    yy, xx, dd = (send(bb, step) for step in (along(dy=1), along(dx=1), along(dx=1, dy=1)))
    got = send(give, swap)
    bb2 = send(bb, swap)
    first2 = send(first, swap)
    q = absorb(span_order, queries.transpose(1, 2, 0), key_absorb, table)
    yy, q = lax.optimization_barrier((yy, q))
    yy2, xx2, dd2 = (send(value, swap) for value in (yy, xx, dd))

    values = attend(span_order, q, value_absorb, (own, first, first2, bb, yy, xx, dd, bb2, yy2, xx2, dd2))
    other = send(values, swap)
    terms = project(values, other, keep, got)
    landed = [
        term if (dx, dy) == (0, 0) else send(term, lambda x, y, z, c, dx=dx, dy=dy: (x + 2 * dx, y + dy, z, c))
        for term, (dx, dy) in zip(terms, OFFSETS)
    ]
    return functools.reduce(jnp.add, [term.astype(F32) for term in landed]).astype(BF16).T


def solution(mesh):
    return jax.shard_map(
        body,
        mesh=mesh,
        in_specs=(
            P("ctx", "head", None),
            P("ctx", None),
            P("head", None, None),
            P("head", None, None),
            P("head", None),
            P(),
        ),
        out_specs=P("ctx", "head"),
        check_vma=False,
    )
```

```python
import functools
import math

import jax
import jax.numpy as jnp
import numpy as np
from jax import lax
from jax.experimental import pallas as pl
from jax.experimental.pallas import tpu as pltpu
from jax.sharding import PartitionSpec as P

BF16 = jnp.bfloat16
F32 = jnp.float32
AXES = ("ctx", "head")
NXL, NZ, NXH, NY, NC = 2, 8, 2, 4, 2
SPAN = 128
LAT = 512
ROPE = 64
KEY = LAT + ROPE
HEADS = 4
NEG = -1e30
MIB = 1024 * 1024


def vmem(mib):
    return pltpu.CompilerParams(vmem_limit_bytes=mib * MIB)


def device(x, y, z, c):
    x, y, z = x % 4, y % NY, z % NZ
    return ((((x % 2) * NZ + z) * NXH + x // 2) * NY + y) * NC + c


def routes(step):
    pairs = []
    for x in range(4):
        for y in range(NY):
            for z in range(NZ):
                for c in range(NC):
                    pairs.append((device(x, y, z, c), device(*step(x, y, z, c))))
    return pairs


def way(c):
    return 1 - 2 * c


def send(value, step):
    return lax.ppermute(value, AXES, routes(step))


def along(dx=0, dy=0, dz=0):
    return lambda x, y, z, c: (x + dx * way(c), y + dy * way(c), z + dz * way(c), c)


def swap(x, y, z, c):
    return x, y, z, 1 - c


def tables():
    inverse = 10000.0 ** (-np.arange(ROPE // 2, dtype=np.float64) * 2.0 / ROPE)[:, None]
    rows = inverse * np.arange(SPAN, dtype=np.float64)[None, :]
    spans = inverse * SPAN * np.arange(SPAN, dtype=np.float64)[None, :]
    return jnp.asarray(np.stack([np.cos(rows), np.sin(rows), np.cos(spans), np.sin(spans)]).astype(np.float32))


def cos_sin(table_ref, span):
    here = lax.broadcasted_iota(jnp.int32, (ROPE // 2, SPAN), 1) == span
    cs = jnp.sum(jnp.where(here, table_ref[2], 0.0), axis=1, keepdims=True)
    ss = jnp.sum(jnp.where(here, table_ref[3], 0.0), axis=1, keepdims=True)
    cr, sr = table_ref[0], table_ref[1]
    return cr * cs - sr * ss, cr * ss + sr * cs


def rotated(values, cos, sin):
    front, back = values[0:32].astype(F32), values[32:64].astype(F32)
    return jnp.concatenate([front * cos - back * sin, front * sin + back * cos], axis=0)


def me():
    ctx, head = lax.axis_index("ctx"), lax.axis_index("head")
    return ctx // NZ, ctx % NZ, head // (NY * NC), (head // NC) % NY, head % NC


def span_of(order_ref, xl, z, half):
    ctx = xl * NZ + lax.rem(z + 2 * NZ, NZ)
    a, b = order_ref[2 * ctx], order_ref[2 * ctx + 1]
    return jnp.where(half == 0, jnp.minimum(a, b), jnp.maximum(a, b))


def own_rows(order_ref, half):
    ctx = lax.axis_index("ctx")
    swapped = (order_ref[2 * ctx] > order_ref[2 * ctx + 1]).astype(jnp.int32)
    return pl.multiple_of(SPAN * (swapped ^ half), SPAN)


SMEM_SPEC = pl.BlockSpec(memory_space=pltpu.SMEM)
VMEM_SPEC = pl.BlockSpec(memory_space=pltpu.VMEM)
ANY_SPEC = pl.BlockSpec(memory_space=pl.ANY)


def pack_kernel(order_ref, cache_any, table_any, own_ref, slice_ref, first_ref, cache_ref, table_ref, sems):
    xl, z, xh, y, c = me()
    loads = (
        pltpu.make_async_copy(table_any, table_ref, sems.at[0]),
        pltpu.make_async_copy(cache_any, cache_ref, sems.at[1]),
    )
    for load in loads:
        load.start()
    for load in loads:
        load.wait()
    for half in range(2):
        tokens = pl.ds(own_rows(order_ref, half), SPAN)
        cos, sin = cos_sin(table_ref, span_of(order_ref, xl, z, half))
        own_ref[half, 0:LAT, :] = cache_ref[0:LAT, tokens]
        own_ref[half, LAT:KEY, :] = rotated(cache_ref[LAT:KEY, tokens], cos, sin).astype(BF16)
    slice_ref[...] = own_ref[y % 2]
    first_ref[...] = own_ref[c]


def pack(order, cache, table):
    return pl.pallas_call(
        pack_kernel,
        out_shape=(
            jax.ShapeDtypeStruct((2, KEY, SPAN), BF16),
            jax.ShapeDtypeStruct((KEY, SPAN), BF16),
            jax.ShapeDtypeStruct((KEY, SPAN), BF16),
        ),
        in_specs=[SMEM_SPEC, ANY_SPEC, ANY_SPEC],
        out_specs=(VMEM_SPEC,) * 3,
        scratch_shapes=[
            pltpu.VMEM((KEY, 2 * SPAN), BF16),
            pltpu.VMEM((4, ROPE // 2, SPAN), F32),
            pltpu.SemaphoreType.DMA((2,)),
        ],
        compiler_params=vmem(60),
        name="pack_keys",
    )(order, cache, table)


def absorb_kernel(order_ref, query_ref, absorb_ref, table_ref, out_ref):
    xl, z, xh, y, c = me()
    for half in range(2):
        tokens = pl.ds(own_rows(order_ref, half), SPAN)
        cos, sin = cos_sin(table_ref, span_of(order_ref, xl, z, half))
        for h in range(HEADS):
            rows = slice(h * SPAN, (h + 1) * SPAN)
            nope = query_ref[h, 0:128, tokens].T
            part = jnp.dot(nope, absorb_ref[h], preferred_element_type=F32)
            out_ref[half, rows, 0:LAT] = part.astype(BF16)
            turned = rotated(query_ref[h, 128:192, tokens], cos, sin)
            out_ref[half, rows, LAT:KEY] = turned.T.astype(BF16)


def absorb(order, queries, key_absorb, table):
    return pl.pallas_call(
        absorb_kernel,
        out_shape=jax.ShapeDtypeStruct((2, HEADS * SPAN, KEY), BF16),
        in_specs=[SMEM_SPEC] + [VMEM_SPEC] * 3,
        out_specs=VMEM_SPEC,
        compiler_params=vmem(16),
        name="absorb_queries",
    )(order, queries, key_absorb, table)


BLOCK = 4
STEPS = 7


HALF = KEY // 2
BUNDLE = 3 * KEY + HALF
SIZES = (2 * KEY,) + (KEY,) + (BUNDLE,) * 4 + (KEY,) + (BUNDLE,) * 4
BASES = tuple(sum(SIZES[:i]) for i in range(len(SIZES) + 1))


def attend_kernel(order_ref, q_ref, va_ref, keys, out_ref, top_row, end_row, scores, peaks, total, acc):
    xl, z, xh, y, c = me()
    s = y % 2
    w = 1 - 2 * c

    def put(span, row, end=None):
        top_row[span] = row
        end_row[span] = row + HALF if end is None else end

    for half in range(2):
        put(span_of(order_ref, xl, z, half), BASES[0] + KEY * half)
    put(span_of(order_ref, 1 - xl, z, c), BASES[1])
    put(span_of(order_ref, 1 - xl, z, 1 - c), BASES[6])
    for k, (px, ph) in enumerate(((xl, s), (xl, 1 - s), (1 - xl, s), (1 - xl, 1 - s))):
        mine, other = BASES[2 + k], BASES[7 + k]
        for t in (1, 2, 3):
            put(span_of(order_ref, px, z - w * t, ph), mine + KEY * (t - 1))
            put(span_of(order_ref, px, z + w * t, ph), other + KEY * (t - 1))
        ends = (mine + 3 * KEY, other + 3 * KEY)
        put(
            span_of(order_ref, px, z + 4, ph),
            jnp.where(c == 0, ends[0], ends[1]),
            jnp.where(c == 0, ends[1], ends[0]),
        )

    lower = span_of(order_ref, xl, z, 0)
    upper = 31 - lower
    count = lower // BLOCK
    scale = math.log2(math.e) / math.sqrt(192.0)
    wide = BLOCK * SPAN

    def tokens(block, rows):
        columns = []
        for i in range(BLOCK):
            top = pl.multiple_of(top_row[BLOCK * block + i], 32)
            end = pl.multiple_of(end_row[BLOCK * block + i], 32)
            parts = [keys[pl.ds(top, HALF), :], keys[pl.ds(end, rows - HALF), :]]
            columns.append(jnp.concatenate(parts, axis=0))
        return jnp.concatenate(columns, axis=1)

    def score(half, block):
        return jnp.dot(q_ref[half], tokens(block, KEY), preferred_element_type=F32)

    def widest(value):
        parts = [value[:, 128 * i : 128 * (i + 1)] for i in range(BLOCK)]
        return jnp.maximum(jnp.maximum(parts[0], parts[1]), jnp.maximum(parts[2], parts[3]))

    def place(i):
        half = (i >= count).astype(jnp.int32)
        return half, i - half * count

    for half, span in ((0, lower), (1, upper)):
        value = score(half, span // BLOCK)
        row = lax.broadcasted_iota(jnp.int32, value.shape, 0) % SPAN + (span % BLOCK) * SPAN
        column = lax.broadcasted_iota(jnp.int32, value.shape, 1)
        value = jnp.where(column <= row, value, NEG)
        scores[STEPS + half] = value
        peaks[STEPS + half] = widest(value)
    for i in range(STEPS):
        value = score(*place(i))
        scores[i] = value
        peaks[i] = widest(value)

    for half in range(2):
        top = peaks[STEPS + half]
        for i in range(STEPS):
            top = jnp.where(place(i)[0] == half, jnp.maximum(top, peaks[i]), top)
        top = jnp.max(top, axis=1, keepdims=True) * scale
        peaks[STEPS + half] = jnp.broadcast_to(top, top.shape[:1] + (128,))

    def weigh(i, half, block):
        top = peaks[STEPS + half]
        parts = [jnp.exp2(scores[i, :, 128 * j : 128 * (j + 1)] * scale - top) for j in range(BLOCK)]
        weights = jnp.concatenate([part.astype(BF16) for part in parts], axis=1)
        product = lax.dot_general(
            weights, tokens(block, LAT), (((1,), (1,)), ((), ())), preferred_element_type=F32
        )
        return (parts[0] + parts[1]) + (parts[2] + parts[3]), product

    for half, span in ((0, lower), (1, upper)):
        total[half], acc[half] = weigh(STEPS + half, half, span // BLOCK)
    for i in range(STEPS):
        half, block = place(i)
        some, product = weigh(i, half, block)
        total[half] += some
        acc[half] += product

    for half in range(2):
        rows = own_rows(order_ref, half)
        for h in range(HEADS):
            part = slice(h * SPAN, (h + 1) * SPAN)
            share = 1.0 / jnp.sum(total[half, part, :], axis=1, keepdims=True)
            context = (acc[half, part, :] * share).astype(BF16)
            value = jnp.dot(context, va_ref[h], preferred_element_type=F32)
            out_ref[pl.ds(rows, SPAN), h * 128 : (h + 1) * 128] = value.astype(BF16)


def attend(order, q, value_absorb, keys):
    rows = HEADS * SPAN
    return pl.pallas_call(
        attend_kernel,
        out_shape=jax.ShapeDtypeStruct((2 * SPAN, HEADS * 128), BF16),
        in_specs=[SMEM_SPEC] + [VMEM_SPEC] * 3,
        out_specs=VMEM_SPEC,
        scratch_shapes=[
            pltpu.SMEM((32,), jnp.int32),
            pltpu.SMEM((32,), jnp.int32),
            pltpu.VMEM((STEPS + 2, rows, BLOCK * SPAN), F32),
            pltpu.VMEM((STEPS + 2, rows, 128), F32),
            pltpu.VMEM((2, rows, 128), F32),
            pltpu.VMEM((2, rows, LAT), F32),
        ],
        compiler_params=vmem(40),
        cost_estimate=pl.CostEstimate(flops=6_000_000_000, bytes_accessed=8_000_000, transcendentals=2_200_000),
        name="attend",
    )(order, q, value_absorb, keys)


def columns_kernel(weight_ref, wait_ref, keep_ref, give_ref):
    c = lax.axis_index("head") % NC
    turned = weight_ref[...].T

    @pl.when(c == 0)
    def _():
        keep_ref[...] = turned[0:448]
        give_ref[...] = turned[448:896]

    @pl.when(c == 1)
    def _():
        keep_ref[...] = turned[448:896]
        give_ref[...] = turned[0:448]


def split_columns(weight, wait):
    rows = weight.shape[0]
    return pl.pallas_call(
        columns_kernel,
        grid=(8,),
        out_shape=(jax.ShapeDtypeStruct((8 * 448, rows), BF16),) * 2,
        in_specs=[pl.BlockSpec((rows, 896), lambda k: (0, k)), ANY_SPEC],
        out_specs=(pl.BlockSpec((448, rows), lambda k: (k, 0)),) * 2,
        compiler_params=vmem(24),
        cost_estimate=pl.CostEstimate(flops=0, bytes_accessed=15_000_000, transcendentals=0),
        name="split_columns",
    )(weight, wait)


OFFSETS = [(1, 2), (1, 1), (1, 3), (1, 0), (0, 2), (0, 1), (0, 3), (0, 0)]


def project_kernel(own_ref, other_ref, keep_ref, got_ref, *outs):
    xl, z, xh, y, c = me()
    contract = (((1,), (1,)), ((), ()))
    for out_ref, (dx, dy) in zip(outs, OFFSETS):
        k = lax.rem(xh + dx, NXH) * NY + lax.rem(y + dy, NY)
        rows = pl.ds(pl.multiple_of(k * 448, 64), 448)
        term = lax.dot_general(keep_ref[rows, :], own_ref[...], contract, preferred_element_type=F32)
        term += lax.dot_general(got_ref[rows, :], other_ref[...], contract, preferred_element_type=F32)
        out_ref[...] = term.astype(BF16)


def project(own, other, keep, got):
    return pl.pallas_call(
        project_kernel,
        out_shape=(jax.ShapeDtypeStruct((448, 256), BF16),) * 8,
        in_specs=[VMEM_SPEC] * 4,
        out_specs=(VMEM_SPEC,) * 8,
        compiler_params=vmem(24),
        cost_estimate=pl.CostEstimate(flops=1_900_000_000, bytes_accessed=8_000_000, transcendentals=0),
        name="project",
    )(own, other, keep, got)


def body(queries, latent_cache, key_absorb, value_absorb, out_weight, span_order):
    table = tables()
    own, piece, first_half = pack(span_order, latent_cache.T, table)

    ways = (along(dy=1), along(dx=1), along(dx=1, dy=1))
    c = lax.axis_index("head") % NC
    b3 = send(piece, along(dz=3))
    b4 = send(jnp.where(c == 0, piece[:HALF], piece[HALF:]), along(dz=4))
    b2 = send(piece, along(dz=2))
    b1 = send(piece, along(dz=1))
    first = send(first_half, along(dx=1))
    keep, give = split_columns(out_weight, piece)
    bundle, give, first = lax.optimization_barrier((jnp.concatenate([b1, b2, b3, b4], axis=0), give, first))
    bundles = [send(bundle, step) for step in (along(dy=1), along(dx=1), along(dx=1, dy=1))]
    got = send(give, swap)
    early = jnp.concatenate([first, bundle], axis=0)
    early2 = send(early, swap)
    early2, queries = lax.optimization_barrier((early2, queries))
    q = absorb(span_order, queries.transpose(1, 2, 0), key_absorb, table)
    bundles[1], q = lax.optimization_barrier((bundles[1], q))
    bundles2 = [send(value, swap) for value in bundles]
    keys = jnp.concatenate([own.reshape(2 * KEY, SPAN), early] + bundles + [early2] + bundles2, axis=0)

    values = attend(span_order, q, value_absorb, keys)
    terms = project(values, send(values, swap), keep, got)

    def deliver(term, dx, dy):
        return send(term, lambda x, y, z, c: (x + 2 * dx, y + dy, z, c))

    landed = [deliver(term, *offset) for term, offset in zip(terms[:5], OFFSETS)]
    rest = lax.optimization_barrier((landed[0], *terms[5:7]))
    landed[0] = rest[0]
    landed += [deliver(term, *offset) for term, offset in zip(rest[1:], OFFSETS[5:])]
    landed.append(terms[7])
    return functools.reduce(jnp.add, [term.astype(F32) for term in landed]).astype(BF16).T


def solution(mesh):
    return jax.shard_map(
        body,
        mesh=mesh,
        in_specs=(
            P("ctx", "head", None),
            P("ctx", None),
            P("head", None, None),
            P("head", None, None),
            P("head", None),
            P(),
        ),
        out_specs=P("ctx", "head"),
        check_vma=False,
    )
```
